32 devices in a mesh: groups: 2 (over y), row: 4 (over z), col: 2 (over x), rep: 2 (over core).
Axes of the slice: x: 2, y: 2, z: 4, core: 2. Of those that a mesh axis runs over, the one named last changes fastest.
Arguments:
- latents: bfloat16 [2048, 128], P(('groups', 'row', 'col', 'rep')), parts along dimension 0, may hold values from -6 to 6
- saved_sum: bfloat16 [2048, 128], P(('groups', 'row', 'col', 'rep')), parts along dimension 0, may hold values from -12 to 12
- grad_latents_out: bfloat16 [2048, 128], P(('groups', 'row', 'col', 'rep')), parts along dimension 0, may hold values from -6 to 6
- edge_latents: bfloat16 [1024, 128, 128], P(('groups', 'row', 'col', 'rep')), parts along dimension 0, may hold values from -6 to 6
- grad_edges_out: bfloat16 [1024, 128, 128], P(('groups', 'row', 'col', 'rep')), parts along dimension 0, may hold values from -6 to 6
- recv_slot: int32 [1024, 128], P(('groups', 'row', 'col', 'rep')), parts along dimension 0, may hold values from -1 to 127
- send_slot: int32 [1024, 128], P(('groups', 'row', 'col', 'rep')), parts along dimension 0, may hold values from 0 to 127
- tile_recv: int32 [1024], P(('groups', 'row', 'col', 'rep')), parts along dimension 0, may hold values from 0 to 3
- tile_send: int32 [1024], P(('groups', 'row', 'col', 'rep')), parts along dimension 0, may hold values from 0 to 1
- tile_count: int32 [32], P(('groups', 'row', 'col', 'rep')), parts along dimension 0, may hold values from 4 to 32, as said below
- edge_first: bfloat16 [384, 128], replicated, may hold values from -0.3125 to 0.3125
- edge_second: bfloat16 [128, 128], replicated, may hold values from -0.5 to 0.5
- edge_gain: float32 [128], replicated, may hold values from 0.5 to 1.5
- node_first: bfloat16 [256, 128], replicated, may hold values from -0.375 to 0.375
- node_second: bfloat16 [128, 128], replicated, may hold values from -0.5 to 0.5
- node_gain: float32 [128], replicated, may hold values from 0.5 to 1.5
Outputs:
- grad_latents: bfloat16 [2048, 128], P(('groups', 'row', 'col', 'rep')), parts along dimension 0
- grad_edges: bfloat16 [1024, 128, 128], P(('groups', 'row', 'col', 'rep')), parts along dimension 0
- grad_edge_first: float32 [768, 128], P('groups'), parts along dimension 0
- grad_edge_second: float32 [256, 128], P('groups'), parts along dimension 0
- grad_edge_gain: float32 [256], P('groups'), parts along dimension 0
- grad_node_first: float32 [512, 128], P('groups'), parts along dimension 0
- grad_node_second: float32 [256, 128], P('groups'), parts along dimension 0
- grad_node_gain: float32 [256], P('groups'), parts along dimension 0
The draws below stay inside these ranges and needn't reach their ends.
There are 2 independent parts, one for each index of `groups`. The reference program is written for one: setup_inputs(seed, part) draws one part's arguments, and reference() takes and returns one part's arrays. A program takes and returns all parts, laid end to end along the dimension named above; an argument that names none is the same for every part. Nothing has to cross between parts.
Inputs may be any that keep to these rules, and one draw needn't show every extreme that they name: tile_count[d] counts the live tiles of device d; they are its first tile slots; each count is 32, 16, 8 or 4, and some device has all 32 live. `recv_slot`: -1 marks an empty edge slot.
All inputs are finite; a program needn't handle non-finite values.
Results may differ from the reference program's by a relative error of at most 0.0067.
Values may be sent and summed in bfloat16 or wider, within the bound.
A program may use at most 64 MiB of HBM per device.

```python
import jax
import jax.numpy as jnp
from jax import lax

D = 128
HID = 128
BLK = 128
ET = 128
NT = 32
P_SIZE = 1024
DEV_PART = 16
TILES = 512
N_ROW = 4
N_COL = 2
N_REP = 2


def draw_tile_count(key, part):
    key = jax.random.fold_in(key, 7)
    shift_key, pick_key = jax.random.split(key)
    shifts = jax.random.randint(shift_key, (DEV_PART,), 0, 4).astype(jnp.int32)
    counts = jnp.right_shift(jnp.full((DEV_PART,), NT, jnp.int32), shifts)
    chosen = jax.random.randint(pick_key, (), 0, DEV_PART).astype(jnp.int32)
    return jnp.where(jnp.arange(DEV_PART, dtype=jnp.int32) == chosen, NT, counts).astype(jnp.int32)


def plant(array, key, low, largest):
    longest = array.shape.index(max(array.shape))
    spots = []
    for shift in (0, 1):
        where = [jax.random.randint(jax.random.fold_in(key, axis), (), 0, length) for axis, length in enumerate(array.shape)]
        where[longest] = (where[longest] + shift) % array.shape[longest]
        spots.append(tuple(where))
    return array.at[spots[0]].set(low).at[spots[1]].set(largest)


def block_levels(stream_key, shape, cuts, low, top_value):
    gain = 1.0
    for position, parts in cuts:
        steps = jax.random.uniform(jax.random.fold_in(jax.random.fold_in(stream_key, 6), position), (parts,), jnp.float32, low / len(cuts), top_value / len(cuts))
        gain = gain * jnp.repeat(jnp.exp(steps), shape[position] // parts).reshape((-1,) + (1,) * (len(shape) - 1 - position))
    return gain


def gaussian(rng, shape, scale, bound, cuts=(), kind=jnp.bfloat16):
    array = scale * jax.random.normal(rng, shape, jnp.float32)
    if cuts:
        array = array * block_levels(rng, shape, cuts, -0.22, 0.18)
    return jnp.clip(array, -bound, bound).astype(kind)


def setup_inputs(seed: int = 0, part: int = 0) -> dict:
    seeds = jax.random.split(jax.random.key(seed), 17)
    part_keys = jax.random.split(jax.random.fold_in(seeds[16], part), 17)
    return {
        "latents": gaussian(part_keys[0], (P_SIZE, D), 1.0, 6.0, ((0, 16),)),
        "saved_sum": gaussian(part_keys[1], (P_SIZE, D), 2.0, 12.0, ((0, 16),)),
        "grad_latents_out": gaussian(part_keys[2], (P_SIZE, D), 1.0, 6.0, ((0, 16),)),
        "edge_latents": gaussian(part_keys[3], (TILES, ET, D), 1.0, 6.0, ((0, 16),)),
        "grad_edges_out": gaussian(part_keys[4], (TILES, ET, D), 1.0, 6.0, ((0, 16),)),
        "recv_slot": plant(jax.random.randint(part_keys[5], (TILES, ET), -1, BLK), jax.random.fold_in(part_keys[5], 1), -1, BLK - 1).astype(jnp.int32),
        "send_slot": plant(jax.random.randint(part_keys[6], (TILES, ET), 0, BLK), jax.random.fold_in(part_keys[6], 1), 0, BLK - 1).astype(jnp.int32),
        "tile_recv": plant(jax.random.randint(part_keys[7], (TILES,), 0, N_ROW), jax.random.fold_in(part_keys[7], 1), 0, N_ROW - 1).astype(jnp.int32),
        "tile_send": plant(jax.random.randint(part_keys[8], (TILES,), 0, N_COL), jax.random.fold_in(part_keys[8], 1), 0, N_COL - 1).astype(jnp.int32),
        "tile_count": draw_tile_count(jax.random.fold_in(jax.random.fold_in(seeds[16], part), 71), part),
        "edge_first": gaussian(seeds[10], (3 * D, HID), (3 * D) ** -0.5, 0.3125),
        "edge_second": gaussian(seeds[11], (HID, D), HID ** -0.5, 0.5),
        "edge_gain": jnp.clip(1.0 + 0.1 * jax.random.normal(seeds[12], (D,), jnp.float32), 0.5, 1.5),
        "node_first": gaussian(seeds[13], (2 * D, HID), (2 * D) ** -0.5, 0.375),
        "node_second": gaussian(seeds[14], (HID, D), HID ** -0.5, 0.5),
        "node_gain": jnp.clip(1.0 + 0.1 * jax.random.normal(seeds[15], (D,), jnp.float32), 0.5, 1.5),
    }


NORM_EPSILON = 1e-05

def layer_norm(raw_out):
    row_mean = lax.optimization_barrier(jnp.mean(raw_out, axis=-1, keepdims=True))
    centred = raw_out - row_mean
    row_var = lax.optimization_barrier(jnp.mean(centred * centred, axis=-1, keepdims=True))
    inv_scale = lax.rsqrt(row_var + NORM_EPSILON)
    return (centred * inv_scale, inv_scale)

def mlp_back(inputs, first_weight, second_weight, gain_vec, upstream, live_mask):
    pre_act = jnp.dot(inputs, first_weight, preferred_element_type=jnp.float32)
    hidden = jnp.maximum(pre_act, 0.0).astype(jnp.bfloat16)
    raw_out = jnp.dot(hidden, second_weight, preferred_element_type=jnp.float32)
    normed, inv_scale = layer_norm(raw_out)
    weighted = upstream * live_mask
    grad_gain = lax.optimization_barrier(jnp.sum(weighted * normed, axis=0))
    scaled = weighted * gain_vec
    grad_raw = inv_scale * (scaled - lax.optimization_barrier(jnp.mean(scaled, axis=-1, keepdims=True)) - normed * lax.optimization_barrier(jnp.mean(scaled * normed, axis=-1, keepdims=True)))
    grad_raw = grad_raw.astype(jnp.bfloat16)
    grad_second = jnp.dot(hidden.T, grad_raw, preferred_element_type=jnp.float32)
    grad_hidden = jnp.dot(grad_raw, second_weight.T, preferred_element_type=jnp.float32)
    grad_pre = jnp.where(pre_act > 0.0, grad_hidden, 0.0).astype(jnp.bfloat16)
    grad_first = jnp.dot(inputs.T, grad_pre, preferred_element_type=jnp.float32)
    grad_inputs = jnp.dot(grad_pre, first_weight.T, preferred_element_type=jnp.float32)
    return (grad_inputs, grad_first, grad_second, grad_gain)

def reference(latents, saved_sum, grad_latents_out, edge_latents, grad_edges_out, recv_slot, send_slot, tile_recv, tile_send, tile_count, edge_first, edge_second, edge_gain, node_first, node_second, node_gain):
    particles = latents.shape[0]
    feat_width = latents.shape[1]
    node_input = jnp.concatenate([latents, saved_sum], axis=1)
    node_live = jnp.ones((particles, 1), jnp.float32)
    grad_node_input, grad_node_first, grad_node_second, grad_node_gain = mlp_back(node_input, node_first, node_second, node_gain, grad_latents_out.astype(jnp.float32), node_live)
    grad_sum = grad_node_input[:, feat_width:].astype(jnp.bfloat16)
    device_count = N_ROW * N_COL * N_REP
    edge_shape = (device_count, NT, ET, feat_width)
    slot_shape = (device_count, NT, ET)
    tile_shape = (device_count, NT)
    tile_numbers = jnp.arange(NT, dtype=jnp.int32)

    def per_device(running, items):
        recv_total, sum_first, sum_second, sum_gain = running
        device_id, edge_block, grad_block, recv_here, send_here, trecv_here, tsend_here, count_here = items
        row_index = device_id // (N_COL * N_REP)
        col_index = device_id // N_REP % N_COL
        live_tiles = tile_numbers < count_here
        live_mask = jnp.logical_and(live_tiles[:, None], recv_here >= 0).astype(jnp.float32).reshape(-1, 1)
        recv_base = (trecv_here * N_COL + col_index) * BLK
        send_base = (row_index * N_COL + tsend_here) * BLK
        recv_rows = (recv_base[:, None] + jnp.maximum(recv_here, 0)).reshape(-1).astype(jnp.int32)
        send_rows = (send_base[:, None] + send_here).reshape(-1).astype(jnp.int32)
        flat_grads = grad_block.reshape(-1, feat_width)
        inputs = jnp.concatenate([edge_block.reshape(-1, feat_width), latents[recv_rows], latents[send_rows]], axis=1)
        upstream = flat_grads.astype(jnp.float32) + grad_sum[recv_rows].astype(jnp.float32)
        grad_inputs, grad_first, grad_second, grad_gain = mlp_back(inputs, edge_first, edge_second, edge_gain, upstream, live_mask)
        new_grads = (flat_grads.astype(jnp.float32) + grad_inputs[:, :feat_width]).astype(jnp.bfloat16)
        pieces = lax.optimization_barrier(grad_inputs[:, feat_width:].astype(jnp.bfloat16)).astype(jnp.float32)
        recv_total = recv_total.at[recv_rows].add(pieces[:, :feat_width])
        recv_total = recv_total.at[send_rows].add(pieces[:, feat_width:])
        running = (recv_total, sum_first + grad_first, sum_second + grad_second, sum_gain + grad_gain)
        return (running, new_grads.reshape(NT, ET, feat_width))
    start = (jnp.zeros((particles, feat_width), jnp.float32), jnp.zeros(edge_first.shape, jnp.float32), jnp.zeros(edge_second.shape, jnp.float32), jnp.zeros((feat_width,), jnp.float32))
    items = (jnp.arange(device_count, dtype=jnp.int32), edge_latents.reshape(edge_shape), grad_edges_out.reshape(edge_shape), recv_slot.reshape(slot_shape), send_slot.reshape(slot_shape), tile_recv.reshape(tile_shape), tile_send.reshape(tile_shape), tile_count)
    finals, grad_edges = lax.scan(per_device, start, items)
    edge_total, grad_edge_first, grad_edge_second, grad_edge_gain = finals
    grad_latents = (grad_latents_out.astype(jnp.float32) + grad_node_input[:, :feat_width] + edge_total).astype(jnp.bfloat16)
    return (grad_latents, grad_edges.reshape(edge_latents.shape), grad_edge_first, grad_edge_second, grad_edge_gain, grad_node_first, grad_node_second, grad_node_gain)
```

```python
import functools

import jax
import jax.numpy as jnp
from jax import lax
from jax.experimental import pallas as pl
from jax.experimental.pallas import tpu as pltpu
from jax.sharding import PartitionSpec as P

NORM_EPSILON = 1e-05
MESH = pl.DeviceIdType.MESH
F32 = jnp.float32
BF16 = jnp.bfloat16
GROUP = 8
PAIR = 2


def dot(a, b):
    return jnp.dot(a, b, preferred_element_type=F32)


def dot_nt(a, b):
    return lax.dot_general(a, b, (((1,), (1,)), ((), ())), preferred_element_type=F32)


def norm_back(raw, weighted, gain):
    row_mean = jnp.mean(raw, axis=-1, keepdims=True)
    centred = raw - row_mean
    row_var = jnp.mean(centred * centred, axis=-1, keepdims=True)
    inv_scale = lax.rsqrt(row_var + NORM_EPSILON)
    normed = centred * inv_scale
    gain_term = weighted * normed
    scaled = weighted * gain
    mean_scaled = jnp.mean(scaled, axis=-1, keepdims=True)
    mean_both = jnp.mean(scaled * normed, axis=-1, keepdims=True)
    grad_raw = inv_scale * (scaled - mean_scaled - normed * mean_both)
    return grad_raw.astype(BF16), gain_term


def node_kernel(
    nr, nc, lat_ref, sum_ref, glo_ref, first_ref, second_ref, gain_ref,
    rlat_ref, rgrad_ref, slat_ref, base_ref, wn_ref,
    gs_buf, lat_send, lat_recv, gs_send, gs_recv, sl_send, sl_recv,
):
    row, col, rep = lax.axis_index("row"), lax.axis_index("col"), lax.axis_index("rep")
    rows, width = lat_ref.shape
    nrr, ncr = nr * 2, nc * 2
    mine_r, mine_c = row * 2 + rep, col * 2 + rep

    def r_dev(k):
        other = lax.rem(mine_r + k, nrr)
        return {"row": lax.div(other, 2), "rep": lax.rem(other, 2)}

    def c_dev(k):
        other = lax.rem(mine_c + k, ncr)
        return {"col": lax.div(other, 2), "rep": lax.rem(other, 2)}

    barrier = pltpu.get_barrier_semaphore()
    for k in range(1, nrr):
        pl.semaphore_signal(barrier, inc=1, device_id=r_dev(k), device_id_type=MESH)
    for k in range(1, ncr):
        pl.semaphore_signal(barrier, inc=1, device_id=c_dev(k), device_id_type=MESH)
    pl.semaphore_wait(barrier, nrr + ncr - 2)

    r_here = pl.ds(pl.multiple_of(mine_r * rows, 16), rows)
    c_here = pl.ds(pl.multiple_of(mine_c * rows, 16), rows)
    lat_copies, sl_copies, gs_copies = [], [], []
    for k in range(1, nrr):
        lat_copies.append(pltpu.make_async_remote_copy(
            src_ref=lat_ref, dst_ref=rlat_ref.at[r_here], send_sem=lat_send.at[k],
            recv_sem=lat_recv.at[k], device_id=r_dev(k), device_id_type=MESH))
        lat_copies[-1].start()
    for k in range(1, ncr):
        sl_copies.append(pltpu.make_async_remote_copy(
            src_ref=lat_ref, dst_ref=slat_ref.at[c_here], send_sem=sl_send.at[k],
            recv_sem=sl_recv.at[k], device_id=c_dev(k), device_id_type=MESH))
        sl_copies[-1].start()

    lat = lat_ref[...]
    inputs = jnp.concatenate([lat, sum_ref[...]], axis=1)
    pre = dot(inputs, first_ref[...])
    hidden = jnp.maximum(pre, 0.0).astype(BF16)
    raw = dot(hidden, second_ref[...])
    upstream = glo_ref[...].astype(F32)
    grad_raw, gain_term = norm_back(raw, upstream, gain_ref[...])
    grad_hidden = dot_nt(grad_raw, second_ref[...])
    grad_pre = jnp.where(pre > 0.0, grad_hidden, 0.0).astype(BF16)
    grad_in = dot_nt(grad_pre, first_ref[...])
    grad_sum = grad_in[:, width:].astype(BF16)
    gs_buf[...] = grad_sum
    for k in range(1, nrr):
        gs_copies.append(pltpu.make_async_remote_copy(
            src_ref=gs_buf, dst_ref=rgrad_ref.at[r_here], send_sem=gs_send.at[k],
            recv_sem=gs_recv.at[k], device_id=r_dev(k), device_id_type=MESH))
        gs_copies[-1].start()
    rlat_ref[r_here, :] = lat
    rgrad_ref[r_here, :] = grad_sum
    slat_ref[c_here, :] = lat
    base_ref[...] = upstream + grad_in[:, :width]
    w1 = first_ref.shape[0]
    w2 = w1 + second_ref.shape[0]
    wn_ref[0:w1, :] = dot(inputs.T, grad_pre).astype(BF16)
    wn_ref[w1:w2, :] = dot(hidden.T, grad_raw).astype(BF16)
    wn_ref[w2:w2 + 16, :] = jnp.broadcast_to(
        jnp.sum(gain_term, axis=0, keepdims=True), (16, width)).astype(BF16)
    for copy in lat_copies + sl_copies + gs_copies:
        copy.wait_recv()
    for copy in lat_copies + sl_copies + gs_copies:
        copy.wait_send()


def edge_kernel(
    nr, nc, half_rows, trecv_ref, tsend_ref, count_ref,
    edge_ref, grad_ref, rslot_ref, sslot_ref, rlat_ref, rgrad_ref, slat_ref,
    first_ref, second_ref, gain_ref, wn_ref,
    out_ref, pack_ref,
    cat, first_t, second_t, acc_r, acc_s, acc_first, acc_second, acc_gain,
):
    step = pl.program_id(0)
    width = edge_ref.shape[2]
    slots = edge_ref.shape[1]
    block = rlat_ref.shape[1]
    count = count_ref[0]

    @pl.when(step == 0)
    def _():
        cat[:, :, 0:width] = rlat_ref[...]
        cat[:, :, width:2 * width] = rgrad_ref[...]
        first_t[...] = first_ref[0:width, :].T
        second_t[...] = second_ref[...].T
        acc_r[...] = jnp.zeros_like(acc_r)
        acc_s[...] = jnp.zeros_like(acc_s)
        acc_first[...] = jnp.zeros_like(acc_first)
        acc_second[...] = jnp.zeros_like(acc_second)
        acc_gain[...] = jnp.zeros_like(acc_gain)

    live_step = step * GROUP < count

    @pl.when(jnp.logical_not(live_step))
    def _():
        out_ref[...] = grad_ref[...]

    @pl.when(live_step)
    def _():
        rcols = rslot_ref[...].T
        scols = sslot_ref[...].T
        lanes = lax.broadcasted_iota(jnp.int32, (slots, block), 1)
        first = first_ref[...]
        gain = gain_ref[...]
        for pair in range(GROUP // PAIR):
            recv_rows, send_rows, weighted, picks, flats = [], [], [], [], []
            for t in range(pair * PAIR, (pair + 1) * PAIR):
                tile = step * GROUP + t
                rcol = jnp.broadcast_to(rcols[:, t:t + 1], (slots, block))
                scol = jnp.broadcast_to(scols[:, t:t + 1], (slots, block))
                rpick = jnp.where(rcol == lanes, 1.0, 0.0).astype(BF16)
                spick = jnp.where(scol == lanes, 1.0, 0.0).astype(BF16)
                from_recv = dot(rpick, cat[trecv_ref[tile]])
                from_send = dot(spick, slat_ref[tsend_ref[tile]])
                recv_rows.append(from_recv[:, 0:width].astype(BF16))
                send_rows.append(from_send.astype(BF16))
                flat = grad_ref[t].astype(F32)
                least = jnp.where(tile < count, 0, block)
                weighted.append(jnp.where(rcol >= least, flat + from_recv[:, width:], 0.0))
                flats.append(flat)
                picks.append(jnp.concatenate([rpick, spick], axis=1))
            edges = edge_ref[pair * PAIR:(pair + 1) * PAIR].reshape(PAIR * slots, width)
            inputs = jnp.concatenate(
                [edges, jnp.concatenate(recv_rows, axis=0), jnp.concatenate(send_rows, axis=0)],
                axis=1)
            pre = dot(inputs, first)
            hidden = jnp.maximum(pre, 0.0).astype(BF16)
            raw = dot(hidden, second_ref[...])
            grad_raw, gain_term = norm_back(raw, jnp.concatenate(weighted, axis=0), gain)
            acc_gain[...] += jnp.sum(gain_term.reshape(-1, 8, width), axis=0)
            grad_hidden = dot(grad_raw, second_t[...])
            grad_pre = jnp.where(pre > 0.0, grad_hidden, 0.0).astype(BF16)
            acc_second[...] += dot(hidden.T, grad_raw)
            grad_in = dot(grad_pre, first_t[...])
            grad_pre_t = grad_pre.T
            acc_first[:, 0:width] += dot(grad_pre_t, edges)
            for i in range(PAIR):
                t = pair * PAIR + i
                tile = step * GROUP + t
                out_ref[t] = (flats[i] + grad_in[i * slots:(i + 1) * slots]).astype(BF16)
                both = dot(grad_pre_t[:, i * slots:(i + 1) * slots], picks[i])
                acc_r[trecv_ref[tile]] += both[:, 0:block]
                acc_s[tsend_ref[tile]] += both[:, block:]

    @pl.when(step == pl.num_programs(0) - 1)
    def _():
        half = block // 2
        recv_w = first_ref[width:2 * width, :]
        send_w = first_ref[2 * width:3 * width, :]
        first_r = acc_first[:, width:2 * width]
        for b in range(nr):
            summed = acc_r[b].astype(BF16)
            total = dot(recv_w, summed).T.astype(BF16)
            first_r += dot(summed, rlat_ref[b])
            for h in range(2):
                pack_ref[h, b * half:(b + 1) * half, :] = total[h * half:(h + 1) * half]
        first_s = acc_first[:, 2 * width:3 * width]
        for b in range(nc):
            summed = acc_s[b].astype(BF16)
            total = dot(send_w, summed).T.astype(BF16)
            first_s += dot(summed, slat_ref[b])
            for h in range(2):
                pack_ref[h, (nr + b) * half:(nr + b + 1) * half, :] = total[h * half:(h + 1) * half]
        w0 = (nr + nc) * half
        hid = second_ref.shape[0]
        pack_ref[0, w0:w0 + width, :] = acc_first[:, 0:width].T.astype(BF16)
        pack_ref[0, w0 + width:w0 + 2 * width, :] = first_r.T.astype(BF16)
        pack_ref[0, w0 + 2 * width:w0 + 3 * width, :] = first_s.T.astype(BF16)
        pack_ref[0, w0 + 3 * width:w0 + 3 * width + hid, :] = acc_second[...].astype(BF16)
        used = 3 * width + hid
        if half_rows > used:
            pack_ref[0, w0 + used:w0 + half_rows, :] = jnp.zeros((half_rows - used, width), BF16)
        nw = wn_ref.shape[0]
        pack_ref[1, w0:w0 + nw, :] = wn_ref[...]
        pack_ref[1, w0 + nw:w0 + nw + 16, :] = jnp.broadcast_to(
            jnp.sum(acc_gain[...], axis=0, keepdims=True), (16, width)).astype(BF16)
        pack_ref[1, w0 + nw + 16:w0 + half_rows, :] = jnp.zeros(
            (half_rows - nw - 16, width), BF16)


def sum_kernel(
    nr, nc, chunk, pack_ref, base_ref,
    glat_ref, ef_ref, es_ref, eg_ref, nf_ref, ns_ref, ng_ref,
    buf, part, rbuf, sbuf, wbuf, wfin,
    p_send, p_recv, w_send, w_recv, r_send, r_recv, s_send, s_recv,
    a_send, a_recv, f_send, f_recv,
):
    row, col, rep = lax.axis_index("row"), lax.axis_index("col"), lax.axis_index("rep")
    chips = nr * nc
    here = row * nc + col
    other_rep = 1 - rep
    rows = base_ref.shape[0]
    w0 = (nr + nc) * rows
    half_rows = chunk * chips
    twin = {"rep": other_rep}

    def chip(k):
        other = lax.rem(here + k, chips)
        return other, {"row": lax.div(other, nc), "col": lax.rem(other, nc)}

    barrier = pltpu.get_barrier_semaphore()
    pl.semaphore_signal(barrier, inc=1, device_id=twin, device_id_type=MESH)
    for k in range(1, chips):
        pl.semaphore_signal(barrier, inc=1, device_id=chip(k)[1], device_id_type=MESH)
    pl.semaphore_wait(barrier, chips)

    def send(src, dst, send_sem, recv_sem, device):
        copy = pltpu.make_async_remote_copy(
            src_ref=src, dst_ref=dst, send_sem=send_sem, recv_sem=recv_sem,
            device_id=device, device_id_type=MESH)
        copy.start()
        return copy

    w_part, n_part = pl.ds(w0, half_rows), pl.ds(0, w0)
    p_w = send(pack_ref.at[other_rep, w_part], buf.at[w_part], p_send.at[0], p_recv.at[0], twin)
    p_n = send(pack_ref.at[other_rep, n_part], buf.at[n_part], p_send.at[1], p_recv.at[1], twin)

    def at_chunk(index):
        return pl.ds(pl.multiple_of(index * chunk, 16), chunk)

    def at_part(offset, index, size):
        return pl.ds(pl.multiple_of(offset + index * size, 16), size)

    p_w.wait_recv()
    part[w_part, :] = (pack_ref[rep, w_part, :].astype(F32) + buf[w_part, :].astype(F32)).astype(BF16)
    w_copies = []
    for k in range(1, chips):
        other, device = chip(k)
        w_copies.append(send(part.at[at_part(w0, other, chunk)], wbuf.at[k],
                             w_send.at[k], w_recv.at[k], device))
    p_n.wait_recv()
    part[n_part, :] = (pack_ref[rep, n_part, :].astype(F32) + buf[n_part, :].astype(F32)).astype(BF16)
    r_copies, s_copies = [], []
    for k in range(1, nr):
        other = lax.rem(row + k, nr)
        r_copies.append(send(part.at[at_part(0, other, rows)], rbuf.at[k],
                             r_send.at[k], r_recv.at[k], {"row": other}))
    for k in range(1, nc):
        other = lax.rem(col + k, nc)
        s_copies.append(send(part.at[at_part(nr * rows, other, rows)], sbuf.at[k],
                             s_send.at[k], s_recv.at[k], {"col": other}))

    total = part[at_part(w0, here, chunk), :].astype(F32)
    for k in range(1, chips):
        w_copies[k - 1].wait_recv()
        total += wbuf[k].astype(F32)
    wfin[rep, at_chunk(here), :] = total.astype(BF16)
    mine = wfin.at[rep, at_chunk(here)]
    a_copies = [send(mine, mine, a_send.at[k], a_recv.at[k], chip(k)[1]) for k in range(1, chips)]
    f_copies = [send(mine, mine, f_send.at[0], f_recv.at[0], twin)]

    grads = base_ref[...] + part[at_part(0, row, rows), :].astype(F32)
    grads += part[at_part(nr * rows, col, rows), :].astype(F32)
    for k in range(1, nr):
        r_copies[k - 1].wait_recv()
        grads += rbuf[k].astype(F32)
    for k in range(1, nc):
        s_copies[k - 1].wait_recv()
        grads += sbuf[k].astype(F32)
    glat_ref[...] = grads.astype(BF16)

    for k in range(1, chips):
        a_copies[k - 1].wait_recv()
        source = lax.rem(here + chips - k, chips)
        passed = wfin.at[rep, at_chunk(source)]
        f_copies.append(send(passed, passed, f_send.at[k], f_recv.at[k], twin))
    for copy in f_copies:
        copy.wait_recv()
    nef, nes = ef_ref.shape[0], es_ref.shape[0]
    ef_ref[...] = wfin[0, 0:nef, :].astype(F32)
    es_ref[...] = wfin[0, nef:nef + nes, :].astype(F32)
    nnf, nns = nf_ref.shape[0], ns_ref.shape[0]
    nf_ref[...] = wfin[1, 0:nnf, :].astype(F32)
    ns_ref[...] = wfin[1, nnf:nnf + nns, :].astype(F32)
    gains = wfin[1, nnf + nns:nnf + nns + 32, :].astype(F32)
    ng_ref[...] = gains[0:1]
    eg_ref[...] = gains[16:17]
    for copy in [p_w, p_n] + w_copies + r_copies + s_copies + a_copies + f_copies:
        copy.wait_send()


def per_device(
    latents, saved_sum, grad_latents_out, edge_latents, grad_edges_out, recv_slot, send_slot,
    tile_recv, tile_send, tile_count, edge_first, edge_second, edge_gain,
    node_first, node_second, node_gain,
):
    nr, nc = lax.axis_size("row"), lax.axis_size("col")
    rows, width = latents.shape
    tiles, slots, _ = edge_latents.shape
    block = rows * 2
    chips = nr * nc
    vmem = pl.BlockSpec(memory_space=pltpu.VMEM)
    dma = pltpu.SemaphoreType.DMA
    weight_rows = edge_first.shape[0] + edge_second.shape[0]
    node_rows = node_first.shape[0] + node_second.shape[0]
    chunk = -(-max(weight_rows, node_rows + 32) // (16 * chips)) * 16
    half_rows = chunk * chips
    nrr, ncr = nr * 2, nc * 2
    shape = jax.ShapeDtypeStruct

    rlat, rgrad, slat, base, wn = pl.pallas_call(
        functools.partial(node_kernel, nr, nc),
        out_shape=(
            shape((nrr * rows, width), BF16), shape((nrr * rows, width), BF16),
            shape((ncr * rows, width), BF16), shape((rows, width), F32),
            shape((node_rows + 16, width), BF16),
        ),
        in_specs=[vmem] * 6,
        out_specs=(vmem,) * 5,
        scratch_shapes=[pltpu.VMEM((rows, width), BF16),
                        dma((nrr,)), dma((nrr,)), dma((nrr,)), dma((nrr,)), dma((ncr,)), dma((ncr,))],
        compiler_params=pltpu.CompilerParams(
            collective_id=0, has_side_effects=True, vmem_limit_bytes=32 << 20),
    )(latents, saved_sum, grad_latents_out, node_first, node_second, node_gain.reshape(1, -1))

    def whole(*dims):
        return pl.BlockSpec(dims, lambda i, *_: (0,) * len(dims))

    tiled = pl.BlockSpec((GROUP, slots, width), lambda i, *_: (i, 0, 0))
    slotted = pl.BlockSpec((GROUP, slots), lambda i, *_: (i, 0))
    pack_rows = (nr + nc) * rows + half_rows
    grads_out, pack = pl.pallas_call(
        functools.partial(edge_kernel, nr, nc, half_rows),
        out_shape=(shape(edge_latents.shape, BF16), shape((2, pack_rows, width), BF16)),
        grid_spec=pltpu.PrefetchScalarGridSpec(
            num_scalar_prefetch=3,
            grid=(tiles // GROUP,),
            in_specs=[
                tiled, tiled, slotted, slotted,
                whole(nr, block, width), whole(nr, block, width), whole(nc, block, width),
                whole(*edge_first.shape), whole(*edge_second.shape), whole(1, width),
                whole(node_rows + 16, width),
            ],
            out_specs=(tiled, whole(2, pack_rows, width)),
            scratch_shapes=[
                pltpu.VMEM((nr, block, 2 * width), BF16),
                pltpu.VMEM((edge_first.shape[1], width), BF16),
                pltpu.VMEM((width, edge_second.shape[0]), BF16),
                pltpu.VMEM((nr, edge_first.shape[1], block), F32),
                pltpu.VMEM((nc, edge_first.shape[1], block), F32),
                pltpu.VMEM((edge_first.shape[1], edge_first.shape[0]), F32),
                pltpu.VMEM(edge_second.shape, F32),
                pltpu.VMEM((8, width), F32),
            ],
        ),
        compiler_params=pltpu.CompilerParams(
            dimension_semantics=("arbitrary",), vmem_limit_bytes=40 << 20),
    )(
        tile_recv, tile_send, tile_count, edge_latents, grad_edges_out, recv_slot, send_slot,
        rlat.reshape(nr, block, width), rgrad.reshape(nr, block, width),
        slat.reshape(nc, block, width), edge_first, edge_second, edge_gain.reshape(1, -1), wn,
    )

    outs = pl.pallas_call(
        functools.partial(sum_kernel, nr, nc, chunk),
        out_shape=(
            shape((rows, width), BF16), shape(edge_first.shape, F32),
            shape(edge_second.shape, F32), shape((1, width), F32),
            shape(node_first.shape, F32), shape(node_second.shape, F32), shape((1, width), F32),
        ),
        in_specs=[vmem] * 2,
        out_specs=(vmem,) * 7,
        scratch_shapes=[
            pltpu.VMEM((pack_rows, width), BF16), pltpu.VMEM((pack_rows, width), BF16),
            pltpu.VMEM((nr, rows, width), BF16), pltpu.VMEM((nc, rows, width), BF16),
            pltpu.VMEM((chips, chunk, width), BF16), pltpu.VMEM((2, half_rows, width), BF16),
            dma((2,)), dma((2,)), dma((chips,)), dma((chips,)), dma((nr,)), dma((nr,)),
            dma((nc,)), dma((nc,)), dma((chips,)), dma((chips,)), dma((chips,)), dma((chips,)),
        ],
        compiler_params=pltpu.CompilerParams(
            collective_id=1, has_side_effects=True, vmem_limit_bytes=40 << 20),
    )(pack, base)
    grad_latents, ef, es, eg, nf, ns, ng = outs
    return (grad_latents, grads_out, ef, es, eg.reshape(-1), nf, ns, ng.reshape(-1))


def solution(mesh):
    spread = ("groups", "row", "col", "rep")
    two, three, one = P(spread, None), P(spread, None, None), P(spread)
    in_specs = (two, two, two, three, three, two, two, one, one, one) + (P(),) * 6
    out_specs = (
        two, three, P("groups", None), P("groups", None), P("groups"),
        P("groups", None), P("groups", None), P("groups"),
    )
    return jax.shard_map(
        per_device, mesh=mesh, in_specs=in_specs, out_specs=out_specs, check_vma=False
    )
```

```python
import functools

import jax
import jax.numpy as jnp
from jax import lax
from jax.experimental import pallas as pl
from jax.experimental.pallas import tpu as pltpu
from jax.sharding import PartitionSpec as P

NORM_EPSILON = 1e-05
MESH = pl.DeviceIdType.MESH
F32 = jnp.float32
BF16 = jnp.bfloat16
GROUP = 8
PAIR = 8
LIMIT = 56 << 20


def dot(a, b):
    return jnp.dot(a, b, preferred_element_type=F32)


def dot_nt(a, b):
    return lax.dot_general(a, b, (((1,), (1,)), ((), ())), preferred_element_type=F32)


def norm_back(raw, weighted, gain):
    row_mean = jnp.mean(raw, axis=-1, keepdims=True)
    centred = raw - row_mean
    row_var = jnp.mean(centred * centred, axis=-1, keepdims=True)
    inv_scale = lax.rsqrt(row_var + NORM_EPSILON)
    normed = centred * inv_scale
    gain_term = weighted * normed
    scaled = weighted * gain
    mean_scaled = jnp.mean(scaled, axis=-1, keepdims=True)
    mean_both = jnp.mean(scaled * normed, axis=-1, keepdims=True)
    grad_raw = inv_scale * (scaled - mean_scaled - normed * mean_both)
    return grad_raw.astype(BF16), gain_term


def node_kernel(
    nr, nc, lat_hbm, sum_hbm, glo_hbm, first_hbm, second_hbm, gain_hbm,
    rlat_ref, rgrad_ref, slat_ref, base_ref, wn_ref,
    lat_ref, sum_ref, glo_ref, first_ref, second_ref, gain_ref, gs_buf, in_sems,
    lat_send, lat_recv, lf_send, lf_recv, gs_send, gs_recv, gf_send, gf_recv,
    sl_send, sl_recv, sf_send, sf_recv,
):
    row, col, rep = lax.axis_index("row"), lax.axis_index("col"), lax.axis_index("rep")
    rows, width = lat_ref.shape
    twin = {"rep": 1 - rep}
    loads = []
    for i, (src, dst) in enumerate((
        (lat_hbm, lat_ref), (sum_hbm, sum_ref), (first_hbm, first_ref),
        (second_hbm, second_ref), (glo_hbm, glo_ref), (gain_hbm, gain_ref),
    )):
        loads.append(pltpu.make_async_copy(src, dst, in_sems.at[i]))
        loads[-1].start()

    def r_dev(k):
        return {"row": lax.rem(row + k, nr)}

    def c_dev(k):
        return {"col": lax.rem(col + k, nc)}

    barrier = pltpu.get_barrier_semaphore()
    pl.semaphore_signal(barrier, inc=1, device_id=twin, device_id_type=MESH)
    for k in range(1, nr):
        pl.semaphore_signal(barrier, inc=1, device_id=r_dev(k), device_id_type=MESH)
    for k in range(1, nc):
        pl.semaphore_signal(barrier, inc=1, device_id=c_dev(k), device_id_type=MESH)
    loads[0].wait()
    pl.semaphore_wait(barrier, nr + nc - 1)

    def send(src, dst, send_sem, recv_sem, device):
        copy = pltpu.make_async_remote_copy(
            src_ref=src, dst_ref=dst, send_sem=send_sem, recv_sem=recv_sem,
            device_id=device, device_id_type=MESH)
        copy.start()
        return copy

    def at(index):
        return pl.ds(pl.multiple_of(index * rows, 16), rows)

    r_here, c_here = at(row * 2 + rep), at(col * 2 + rep)
    lats = [send(lat_ref, rlat_ref.at[r_here], lat_send.at[k], lat_recv.at[k], r_dev(k))
            for k in range(1, nr)]
    slats = [send(lat_ref, slat_ref.at[c_here], sl_send.at[k], sl_recv.at[k], c_dev(k))
             for k in range(1, nc)]
    passed = [send(lat_ref, rlat_ref.at[r_here], lf_send.at[0], lf_recv.at[0], twin),
              send(lat_ref, slat_ref.at[c_here], sf_send.at[0], sf_recv.at[0], twin)]

    for load in loads[1:]:
        load.wait()
    lat = lat_ref[...]
    inputs = jnp.concatenate([lat, sum_ref[...]], axis=1)
    pre = dot(inputs, first_ref[...])
    hidden = jnp.maximum(pre, 0.0).astype(BF16)
    raw = dot(hidden, second_ref[...])
    upstream = glo_ref[...].astype(F32)
    grad_raw, gain_term = norm_back(raw, upstream, gain_ref[...])
    grad_hidden = dot_nt(grad_raw, second_ref[...])
    grad_pre = jnp.where(pre > 0.0, grad_hidden, 0.0).astype(BF16)
    grad_sum = dot_nt(grad_pre, first_ref[width:, :]).astype(BF16)
    gs_buf[...] = grad_sum
    grads = [send(gs_buf, rgrad_ref.at[r_here], gs_send.at[k], gs_recv.at[k], r_dev(k))
             for k in range(1, nr)]
    passed.append(send(gs_buf, rgrad_ref.at[r_here], gf_send.at[0], gf_recv.at[0], twin))
    for k in range(1, nr):
        lats[k - 1].wait_recv()
        block = rlat_ref.at[at(lax.rem(row + nr - k, nr) * 2 + rep)]
        passed.append(send(block, block, lf_send.at[k], lf_recv.at[k], twin))
    for k in range(1, nc):
        slats[k - 1].wait_recv()
        block = slat_ref.at[at(lax.rem(col + nc - k, nc) * 2 + rep)]
        passed.append(send(block, block, sf_send.at[k], sf_recv.at[k], twin))
    rlat_ref[r_here, :] = lat
    rgrad_ref[r_here, :] = grad_sum
    slat_ref[c_here, :] = lat
    base_ref[...] = upstream + dot_nt(grad_pre, first_ref[0:width, :])
    w1 = first_ref.shape[0]
    w2 = w1 + second_ref.shape[0]
    wn_ref[0:w1, :] = dot(inputs.T, grad_pre).astype(BF16)
    wn_ref[w1:w2, :] = dot(hidden.T, grad_raw).astype(BF16)
    wn_ref[w2:w2 + 16, :] = jnp.broadcast_to(
        jnp.sum(gain_term, axis=0, keepdims=True), (16, width)).astype(BF16)
    for k in range(1, nr):
        grads[k - 1].wait_recv()
        block = rgrad_ref.at[at(lax.rem(row + nr - k, nr) * 2 + rep)]
        passed.append(send(block, block, gf_send.at[k], gf_recv.at[k], twin))
    for copy in passed:
        copy.wait_recv()
    for copy in lats + slats + grads + passed:
        copy.wait_send()


def edge_kernel(
    nr, nc, half_rows, trecv_ref, tsend_ref, count_ref,
    edge_ref, grad_ref, rslot_ref, sslot_ref, rlat_ref, rgrad_ref, slat_ref,
    first_ref, second_ref, gain_ref, wn_ref,
    out_ref, pack_ref,
    cat, first_t, second_t, acc_r, acc_s, acc_first, acc_second, acc_gain,
):
    step = pl.program_id(0)
    width = edge_ref.shape[2]
    slots = edge_ref.shape[1]
    block = rlat_ref.shape[1]
    count = count_ref[0]

    @pl.when(step == 0)
    def _():
        cat[:, :, 0:width] = rlat_ref[...]
        cat[:, :, width:2 * width] = rgrad_ref[...]
        first_t[...] = first_ref[0:width, :].T
        second_t[...] = second_ref[...].T
        acc_r[...] = jnp.zeros_like(acc_r)
        acc_s[...] = jnp.zeros_like(acc_s)
        acc_first[...] = jnp.zeros_like(acc_first)
        acc_second[...] = jnp.zeros_like(acc_second)
        acc_gain[...] = jnp.zeros_like(acc_gain)

    live_step = step * GROUP < count

    @pl.when(jnp.logical_not(live_step))
    def _():
        out_ref[...] = grad_ref[...]

    @pl.when(live_step)
    def _():
        rcols = rslot_ref[...].T
        scols = sslot_ref[...].T
        lanes = lax.broadcasted_iota(jnp.int32, (slots, block), 1)
        first = first_ref[...]
        gain = gain_ref[...]
        for pair in range(GROUP // PAIR):
            recv_rows, send_rows, weighted, picks, flats = [], [], [], [], []
            for t in range(pair * PAIR, (pair + 1) * PAIR):
                tile = step * GROUP + t
                rcol = jnp.broadcast_to(rcols[:, t:t + 1], (slots, block))
                scol = jnp.broadcast_to(scols[:, t:t + 1], (slots, block))
                rpick = jnp.where(rcol == lanes, 1.0, 0.0).astype(BF16)
                spick = jnp.where(scol == lanes, 1.0, 0.0).astype(BF16)
                from_recv = dot(rpick, cat[trecv_ref[tile]])
                from_send = dot(spick, slat_ref[tsend_ref[tile]])
                recv_rows.append(from_recv[:, 0:width].astype(BF16))
                send_rows.append(from_send.astype(BF16))
                flat = grad_ref[t].astype(F32)
                least = jnp.where(tile < count, 0, block)
                weighted.append(jnp.where(rcol >= least, flat + from_recv[:, width:], 0.0))
                flats.append(flat)
                picks.append(jnp.concatenate([rpick, spick], axis=1))
            edges = edge_ref[pair * PAIR:(pair + 1) * PAIR].reshape(PAIR * slots, width)
            inputs = jnp.concatenate(
                [edges, jnp.concatenate(recv_rows, axis=0), jnp.concatenate(send_rows, axis=0)],
                axis=1)
            pre = dot(inputs, first)
            hidden = jnp.maximum(pre, 0.0).astype(BF16)
            raw = dot(hidden, second_ref[...])
            grad_raw, gain_term = norm_back(raw, jnp.concatenate(weighted, axis=0), gain)
            acc_gain[...] += jnp.sum(gain_term.reshape(-1, 8, width), axis=0)
            grad_hidden = dot(grad_raw, second_t[...])
            grad_pre = jnp.where(pre > 0.0, grad_hidden, 0.0).astype(BF16)
            acc_second[...] += dot(hidden.T, grad_raw)
            grad_in = dot(grad_pre, first_t[...])
            grad_pre_t = grad_pre.T
            acc_first[:, 0:width] += dot(grad_pre_t, edges)
            for i in range(PAIR):
                t = pair * PAIR + i
                tile = step * GROUP + t
                out_ref[t] = (flats[i] + grad_in[i * slots:(i + 1) * slots]).astype(BF16)
                both = dot(grad_pre_t[:, i * slots:(i + 1) * slots], picks[i])
                acc_r[trecv_ref[tile]] += both[:, 0:block]
                acc_s[tsend_ref[tile]] += both[:, block:]

    @pl.when(step == pl.num_programs(0) - 1)
    def _():
        half = block // 2
        recv_w = first_ref[width:2 * width, :]
        send_w = first_ref[2 * width:3 * width, :]
        first_r = acc_first[:, width:2 * width]
        for b in range(nr):
            summed = acc_r[b].astype(BF16)
            total = dot(recv_w, summed).T.astype(BF16)
            first_r += dot(summed, rlat_ref[b])
            for h in range(2):
                pack_ref[h, b * half:(b + 1) * half, :] = total[h * half:(h + 1) * half]
        first_s = acc_first[:, 2 * width:3 * width]
        for b in range(nc):
            summed = acc_s[b].astype(BF16)
            total = dot(send_w, summed).T.astype(BF16)
            first_s += dot(summed, slat_ref[b])
            for h in range(2):
                pack_ref[h, (nr + b) * half:(nr + b + 1) * half, :] = total[h * half:(h + 1) * half]
        w0 = (nr + nc) * half
        hid = second_ref.shape[0]
        pack_ref[0, w0:w0 + width, :] = acc_first[:, 0:width].T.astype(BF16)
        pack_ref[0, w0 + width:w0 + 2 * width, :] = first_r.T.astype(BF16)
        pack_ref[0, w0 + 2 * width:w0 + 3 * width, :] = first_s.T.astype(BF16)
        pack_ref[0, w0 + 3 * width:w0 + 3 * width + hid, :] = acc_second[...].astype(BF16)
        used = 3 * width + hid
        if half_rows > used:
            pack_ref[0, w0 + used:w0 + half_rows, :] = jnp.zeros((half_rows - used, width), BF16)
        nw = wn_ref.shape[0]
        pack_ref[1, w0:w0 + nw, :] = wn_ref[...]
        pack_ref[1, w0 + nw:w0 + nw + 16, :] = jnp.broadcast_to(
            jnp.sum(acc_gain[...], axis=0, keepdims=True), (16, width)).astype(BF16)
        pack_ref[1, w0 + nw + 16:w0 + half_rows, :] = jnp.zeros(
            (half_rows - nw - 16, width), BF16)


def sum_kernel(
    nr, nc, chunk, pack_ref, base_ref,
    glat_ref, wfin,
    buf, part, rbuf, sbuf, wbuf,
    p_send, p_recv, w_send, w_recv, r_send, r_recv, s_send, s_recv,
    a_send, a_recv, f_send, f_recv,
):
    row, col, rep = lax.axis_index("row"), lax.axis_index("col"), lax.axis_index("rep")
    chips = nr * nc
    here = row * nc + col
    other_rep = 1 - rep
    rows = base_ref.shape[0]
    w0 = (nr + nc) * rows
    half_rows = chunk * chips
    twin = {"rep": other_rep}

    def chip(k):
        other = lax.rem(here + k, chips)
        return other, {"row": lax.div(other, nc), "col": lax.rem(other, nc)}

    barrier = pltpu.get_barrier_semaphore()
    pl.semaphore_signal(barrier, inc=1, device_id=twin, device_id_type=MESH)
    for k in range(1, chips):
        pl.semaphore_signal(barrier, inc=1, device_id=chip(k)[1], device_id_type=MESH)
    pl.semaphore_wait(barrier, chips)

    def send(src, dst, send_sem, recv_sem, device):
        copy = pltpu.make_async_remote_copy(
            src_ref=src, dst_ref=dst, send_sem=send_sem, recv_sem=recv_sem,
            device_id=device, device_id_type=MESH)
        copy.start()
        return copy

    w_part, n_part = pl.ds(w0, half_rows), pl.ds(0, w0)
    p_w = send(pack_ref.at[other_rep, w_part], buf.at[w_part], p_send.at[0], p_recv.at[0], twin)
    p_n = send(pack_ref.at[other_rep, n_part], buf.at[n_part], p_send.at[1], p_recv.at[1], twin)

    def at_chunk(index):
        return pl.ds(pl.multiple_of(index * chunk, 16), chunk)

    def at_part(offset, index, size):
        return pl.ds(pl.multiple_of(offset + index * size, 16), size)

    p_w.wait_recv()
    part[w_part, :] = (pack_ref[rep, w_part, :].astype(F32) + buf[w_part, :].astype(F32)).astype(BF16)
    w_copies = []
    for k in range(1, chips):
        other, device = chip(k)
        w_copies.append(send(part.at[at_part(w0, other, chunk)], wbuf.at[k],
                             w_send.at[k], w_recv.at[k], device))
    p_n.wait_recv()
    part[n_part, :] = (pack_ref[rep, n_part, :].astype(F32) + buf[n_part, :].astype(F32)).astype(BF16)
    r_copies, s_copies = [], []
    for k in range(1, nr):
        other = lax.rem(row + k, nr)
        r_copies.append(send(part.at[at_part(0, other, rows)], rbuf.at[k],
                             r_send.at[k], r_recv.at[k], {"row": other}))
    for k in range(1, nc):
        other = lax.rem(col + k, nc)
        s_copies.append(send(part.at[at_part(nr * rows, other, rows)], sbuf.at[k],
                             s_send.at[k], s_recv.at[k], {"col": other}))

    total = part[at_part(w0, here, chunk), :].astype(F32)
    for k in range(1, chips):
        w_copies[k - 1].wait_recv()
        total += wbuf[k].astype(F32)
    wfin[rep, at_chunk(here), :] = total.astype(BF16)
    mine = wfin.at[rep, at_chunk(here)]
    a_copies = [send(mine, mine, a_send.at[k], a_recv.at[k], chip(k)[1]) for k in range(1, chips)]
    f_copies = [send(mine, mine, f_send.at[0], f_recv.at[0], twin)]

    grads = base_ref[...] + part[at_part(0, row, rows), :].astype(F32)
    grads += part[at_part(nr * rows, col, rows), :].astype(F32)
    for k in range(1, nr):
        r_copies[k - 1].wait_recv()
        grads += rbuf[k].astype(F32)
    for k in range(1, nc):
        s_copies[k - 1].wait_recv()
        grads += sbuf[k].astype(F32)
    glat_ref[...] = grads.astype(BF16)

    for k in range(1, chips):
        a_copies[k - 1].wait_recv()
        source = lax.rem(here + chips - k, chips)
        passed = wfin.at[rep, at_chunk(source)]
        f_copies.append(send(passed, passed, f_send.at[k], f_recv.at[k], twin))
    for copy in f_copies:
        copy.wait_recv()
    for copy in [p_w, p_n] + w_copies + r_copies + s_copies + a_copies + f_copies:
        copy.wait_send()


def write_kernel(
    glat_ref, wfin, glat_out, ef_out, es_out, eg_out, nf_out, ns_out, ng_out,
    ef_ref, es_ref, eg_ref, nf_ref, ns_ref, ng_ref, sems,
):
    def store(i, src, dst):
        copy = pltpu.make_async_copy(src, dst, sems.at[i])
        copy.start()
        return copy

    copies = [store(0, glat_ref, glat_out)]
    nef, nes = ef_ref.shape[0], es_ref.shape[0]
    ef_ref[...] = wfin[0, 0:nef, :].astype(F32)
    copies.append(store(1, ef_ref, ef_out))
    es_ref[...] = wfin[0, nef:nef + nes, :].astype(F32)
    copies.append(store(2, es_ref, es_out))
    nnf, nns = nf_ref.shape[0], ns_ref.shape[0]
    nf_ref[...] = wfin[1, 0:nnf, :].astype(F32)
    copies.append(store(3, nf_ref, nf_out))
    ns_ref[...] = wfin[1, nnf:nnf + nns, :].astype(F32)
    copies.append(store(4, ns_ref, ns_out))
    gains = wfin[1, nnf + nns:nnf + nns + 32, :].astype(F32)
    ng_ref[...] = gains[0:1]
    eg_ref[...] = gains[16:17]
    copies.append(store(5, ng_ref, ng_out))
    copies.append(store(6, eg_ref, eg_out))
    for copy in copies:
        copy.wait()


def per_device(
    latents, saved_sum, grad_latents_out, edge_latents, grad_edges_out, recv_slot, send_slot,
    tile_recv, tile_send, tile_count, edge_first, edge_second, edge_gain,
    node_first, node_second, node_gain,
):
    nr, nc = lax.axis_size("row"), lax.axis_size("col")
    rows, width = latents.shape
    tiles, slots, _ = edge_latents.shape
    block = rows * 2
    chips = nr * nc
    vmem = pl.BlockSpec(memory_space=pltpu.VMEM)
    hbm = pl.BlockSpec(memory_space=pl.ANY)
    dma = pltpu.SemaphoreType.DMA
    weight_rows = edge_first.shape[0] + edge_second.shape[0]
    node_rows = node_first.shape[0] + node_second.shape[0]
    chunk = -(-max(weight_rows, node_rows + 32) // (16 * chips)) * 16
    half_rows = chunk * chips
    shape = jax.ShapeDtypeStruct

    rlat, rgrad, slat, base, wn = pl.pallas_call(
        functools.partial(node_kernel, nr, nc),
        out_shape=(
            shape((nr * block, width), BF16), shape((nr * block, width), BF16),
            shape((nc * block, width), BF16), shape((rows, width), F32),
            shape((node_rows + 16, width), BF16),
        ),
        in_specs=[hbm] * 6,
        out_specs=(vmem,) * 5,
        scratch_shapes=[
            pltpu.VMEM((rows, width), BF16), pltpu.VMEM((rows, width), BF16),
            pltpu.VMEM((rows, width), BF16), pltpu.VMEM(node_first.shape, BF16),
            pltpu.VMEM(node_second.shape, BF16), pltpu.VMEM((1, width), F32),
            pltpu.VMEM((rows, width), BF16), dma((6,)),
        ] + [dma((nr,))] * 8 + [dma((nc,))] * 4,
        compiler_params=pltpu.CompilerParams(
            collective_id=0, has_side_effects=True, vmem_limit_bytes=LIMIT),
    )(latents, saved_sum, grad_latents_out, node_first, node_second, node_gain.reshape(1, -1))

    def whole(*dims):
        return pl.BlockSpec(dims, lambda i, *_: (0,) * len(dims))

    tiled = pl.BlockSpec((GROUP, slots, width), lambda i, *_: (i, 0, 0))
    slotted = pl.BlockSpec((GROUP, slots), lambda i, *_: (i, 0))
    pack_rows = (nr + nc) * rows + half_rows
    grads_out, pack = pl.pallas_call(
        functools.partial(edge_kernel, nr, nc, half_rows),
        out_shape=(shape(edge_latents.shape, BF16), shape((2, pack_rows, width), BF16)),
        grid_spec=pltpu.PrefetchScalarGridSpec(
            num_scalar_prefetch=3,
            grid=(tiles // GROUP,),
            in_specs=[
                tiled, tiled, slotted, slotted,
                whole(nr, block, width), whole(nr, block, width), whole(nc, block, width),
                whole(*edge_first.shape), whole(*edge_second.shape), whole(1, width),
                whole(node_rows + 16, width),
            ],
            out_specs=(tiled, whole(2, pack_rows, width)),
            scratch_shapes=[
                pltpu.VMEM((nr, block, 2 * width), BF16),
                pltpu.VMEM((edge_first.shape[1], width), BF16),
                pltpu.VMEM((width, edge_second.shape[0]), BF16),
                pltpu.VMEM((nr, edge_first.shape[1], block), F32),
                pltpu.VMEM((nc, edge_first.shape[1], block), F32),
                pltpu.VMEM((edge_first.shape[1], edge_first.shape[0]), F32),
                pltpu.VMEM(edge_second.shape, F32),
                pltpu.VMEM((8, width), F32),
            ],
        ),
        compiler_params=pltpu.CompilerParams(
            dimension_semantics=("arbitrary",), vmem_limit_bytes=LIMIT),
    )(
        tile_recv, tile_send, tile_count, edge_latents, grad_edges_out, recv_slot, send_slot,
        rlat.reshape(nr, block, width), rgrad.reshape(nr, block, width),
        slat.reshape(nc, block, width), edge_first, edge_second, edge_gain.reshape(1, -1), wn,
    )

    glat, totals = pl.pallas_call(
        functools.partial(sum_kernel, nr, nc, chunk),
        out_shape=(shape((rows, width), BF16), shape((2, half_rows, width), BF16)),
        in_specs=[vmem] * 2,
        out_specs=(vmem,) * 2,
        scratch_shapes=[
            pltpu.VMEM((pack_rows, width), BF16), pltpu.VMEM((pack_rows, width), BF16),
            pltpu.VMEM((nr, rows, width), BF16), pltpu.VMEM((nc, rows, width), BF16),
            pltpu.VMEM((chips, chunk, width), BF16),
            dma((2,)), dma((2,)), dma((chips,)), dma((chips,)), dma((nr,)), dma((nr,)),
            dma((nc,)), dma((nc,)), dma((chips,)), dma((chips,)), dma((chips,)), dma((chips,)),
        ],
        compiler_params=pltpu.CompilerParams(
            collective_id=1, has_side_effects=True, vmem_limit_bytes=LIMIT),
    )(pack, base)
    finals = (
        shape(edge_first.shape, F32), shape(edge_second.shape, F32), shape((1, width), F32),
        shape(node_first.shape, F32), shape(node_second.shape, F32), shape((1, width), F32),
    )
    outs = pl.pallas_call(
        write_kernel,
        out_shape=(shape((rows, width), BF16),) + finals,
        in_specs=[vmem] * 2,
        out_specs=(hbm,) * 7,
        scratch_shapes=[pltpu.VMEM(item.shape, F32) for item in finals] + [dma((7,))],
        compiler_params=pltpu.CompilerParams(vmem_limit_bytes=LIMIT),
    )(glat, totals)
    grad_latents, ef, es, eg, nf, ns, ng = outs
    return (grad_latents, grads_out, ef, es, eg.reshape(-1), nf, ns, ng.reshape(-1))


def solution(mesh):
    spread = ("groups", "row", "col", "rep")
    two, three, one = P(spread, None), P(spread, None, None), P(spread)
    in_specs = (two, two, two, three, three, two, two, one, one, one) + (P(),) * 6
    out_specs = (
        two, three, P("groups", None), P("groups", None), P("groups"),
        P("groups", None), P("groups", None), P("groups"),
    )
    return jax.shard_map(
        per_device, mesh=mesh, in_specs=in_specs, out_specs=out_specs, check_vma=False
    )
```

```python
import functools

import jax
import jax.numpy as jnp
from jax import lax
from jax.experimental import pallas as pl
from jax.experimental.pallas import tpu as pltpu
from jax.sharding import PartitionSpec as P

NORM_EPSILON = 1e-05
MESH = pl.DeviceIdType.MESH
F32 = jnp.float32
BF16 = jnp.bfloat16
GROUP = 16
PAIR = 8
LIMIT = 56 << 20


def dot(a, b):
    return jnp.dot(a, b, preferred_element_type=F32)


def dot_nt(a, b):
    return lax.dot_general(a, b, (((1,), (1,)), ((), ())), preferred_element_type=F32)


def norm_back(raw, weighted, gain):
    row_mean = jnp.mean(raw, axis=-1, keepdims=True)
    centred = raw - row_mean
    row_var = jnp.mean(centred * centred, axis=-1, keepdims=True)
    inv_scale = lax.rsqrt(row_var + NORM_EPSILON)
    normed = centred * inv_scale
    gain_term = weighted * normed
    scaled = weighted * gain
    mean_scaled = jnp.mean(scaled, axis=-1, keepdims=True)
    mean_both = jnp.mean(scaled * normed, axis=-1, keepdims=True)
    grad_raw = inv_scale * (scaled - mean_scaled - normed * mean_both)
    return grad_raw.astype(BF16), gain_term


def node_kernel(
    nr, nc, lat_hbm, sum_hbm, glo_hbm, first_hbm, second_hbm, gain_hbm,
    rlat_ref, rgrad_ref, slat_ref, base_ref, wn_ref,
    lat_ref, sum_ref, glo_ref, first_ref, second_ref, gain_ref, gs_buf, in_sems,
    lat_send, lat_recv, lf_send, lf_recv, gs_send, gs_recv, gf_send, gf_recv,
    sl_send, sl_recv, sf_send, sf_recv,
):
    row, col, rep = lax.axis_index("row"), lax.axis_index("col"), lax.axis_index("rep")
    rows, width = lat_ref.shape
    twin = {"rep": 1 - rep}
    loads = []
    for i, (src, dst) in enumerate((
        (lat_hbm, lat_ref), (sum_hbm, sum_ref), (first_hbm, first_ref),
        (second_hbm, second_ref), (glo_hbm, glo_ref), (gain_hbm, gain_ref),
    )):
        loads.append(pltpu.make_async_copy(src, dst, in_sems.at[i]))
        loads[-1].start()

    def r_dev(k):
        return {"row": lax.rem(row + k, nr)}

    def c_dev(k):
        return {"col": lax.rem(col + k, nc)}

    barrier = pltpu.get_barrier_semaphore()
    pl.semaphore_signal(barrier, inc=1, device_id=twin, device_id_type=MESH)
    for k in range(1, nr):
        pl.semaphore_signal(barrier, inc=1, device_id=r_dev(k), device_id_type=MESH)
    for k in range(1, nc):
        pl.semaphore_signal(barrier, inc=1, device_id=c_dev(k), device_id_type=MESH)
    loads[0].wait()
    pl.semaphore_wait(barrier, nr + nc - 1)

    def send(src, dst, send_sem, recv_sem, device):
        copy = pltpu.make_async_remote_copy(
            src_ref=src, dst_ref=dst, send_sem=send_sem, recv_sem=recv_sem,
            device_id=device, device_id_type=MESH)
        copy.start()
        return copy

    def at(index):
        return pl.ds(pl.multiple_of(index * rows, 16), rows)

    r_here, c_here = at(row * 2 + rep), at(col * 2 + rep)
    lats = [send(lat_ref, rlat_ref.at[r_here], lat_send.at[k], lat_recv.at[k], r_dev(k))
            for k in range(1, nr)]
    slats = [send(lat_ref, slat_ref.at[c_here], sl_send.at[k], sl_recv.at[k], c_dev(k))
             for k in range(1, nc)]
    passed = [send(lat_ref, rlat_ref.at[r_here], lf_send.at[0], lf_recv.at[0], twin),
              send(lat_ref, slat_ref.at[c_here], sf_send.at[0], sf_recv.at[0], twin)]

    for load in loads[1:]:
        load.wait()
    lat = lat_ref[...]
    inputs = jnp.concatenate([lat, sum_ref[...]], axis=1)
    pre = dot(inputs, first_ref[...])
    hidden = jnp.maximum(pre, 0.0).astype(BF16)
    raw = dot(hidden, second_ref[...])
    upstream = glo_ref[...].astype(F32)
    grad_raw, gain_term = norm_back(raw, upstream, gain_ref[...])
    grad_hidden = dot_nt(grad_raw, second_ref[...])
    grad_pre = jnp.where(pre > 0.0, grad_hidden, 0.0).astype(BF16)
    grad_sum = dot_nt(grad_pre, first_ref[width:, :]).astype(BF16)
    gs_buf[...] = grad_sum
    grads = [send(gs_buf, rgrad_ref.at[r_here], gs_send.at[k], gs_recv.at[k], r_dev(k))
             for k in range(1, nr)]
    passed.append(send(gs_buf, rgrad_ref.at[r_here], gf_send.at[0], gf_recv.at[0], twin))
    for k in range(1, nr):
        lats[k - 1].wait_recv()
        block = rlat_ref.at[at(lax.rem(row + nr - k, nr) * 2 + rep)]
        passed.append(send(block, block, lf_send.at[k], lf_recv.at[k], twin))
    for k in range(1, nc):
        slats[k - 1].wait_recv()
        block = slat_ref.at[at(lax.rem(col + nc - k, nc) * 2 + rep)]
        passed.append(send(block, block, sf_send.at[k], sf_recv.at[k], twin))
    rlat_ref[r_here, :] = lat
    rgrad_ref[r_here, :] = grad_sum
    slat_ref[c_here, :] = lat
    base_ref[...] = upstream + dot_nt(grad_pre, first_ref[0:width, :])
    w1 = first_ref.shape[0]
    w2 = w1 + second_ref.shape[0]
    wn_ref[0:w1, :] = dot(inputs.T, grad_pre).astype(BF16)
    wn_ref[w1:w2, :] = dot(hidden.T, grad_raw).astype(BF16)
    wn_ref[w2:w2 + 16, :] = jnp.broadcast_to(
        jnp.sum(gain_term, axis=0, keepdims=True), (16, width)).astype(BF16)
    for k in range(1, nr):
        grads[k - 1].wait_recv()
        block = rgrad_ref.at[at(lax.rem(row + nr - k, nr) * 2 + rep)]
        passed.append(send(block, block, gf_send.at[k], gf_recv.at[k], twin))
    for copy in passed:
        copy.wait_recv()
    for copy in lats + slats + grads + passed:
        copy.wait_send()


def edge_kernel(
    nr, nc, half_rows, trecv_ref, tsend_ref, count_ref,
    edge_ref, grad_ref, rslot_ref, sslot_ref, rlat_ref, rgrad_ref, slat_ref,
    first_ref, second_ref, gain_ref, wn_ref,
    out_ref, pack_ref,
    cat, first_t, second_t, acc_r, acc_s, acc_first, acc_second, acc_gain,
):
    step = pl.program_id(0)
    width = edge_ref.shape[2]
    slots = edge_ref.shape[1]
    block = rlat_ref.shape[1]
    count = count_ref[0]

    @pl.when(step == 0)
    def _():
        cat[:, :, 0:width] = rlat_ref[...]
        cat[:, :, width:2 * width] = rgrad_ref[...]
        first_t[...] = first_ref[0:width, :].T
        second_t[...] = second_ref[...].T
        acc_r[...] = jnp.zeros_like(acc_r)
        acc_s[...] = jnp.zeros_like(acc_s)
        acc_first[...] = jnp.zeros_like(acc_first)
        acc_second[...] = jnp.zeros_like(acc_second)
        acc_gain[...] = jnp.zeros_like(acc_gain)

    live_step = step * GROUP < count

    @pl.when(jnp.logical_not(live_step))
    def _():
        out_ref[...] = grad_ref[...]

    @pl.when(live_step)
    def _():
        rcols = rslot_ref[...].T
        scols = sslot_ref[...].T
        lanes = lax.broadcasted_iota(jnp.int32, (slots, block), 1)
        first = first_ref[...]
        gain = gain_ref[...]
        for pair in range(GROUP // PAIR):
            recv_rows, send_rows, weighted, picks, flats = [], [], [], [], []
            for t in range(pair * PAIR, (pair + 1) * PAIR):
                tile = step * GROUP + t
                rcol = jnp.broadcast_to(rcols[:, t:t + 1], (slots, block))
                scol = jnp.broadcast_to(scols[:, t:t + 1], (slots, block))
                rpick = jnp.where(rcol == lanes, 1.0, 0.0).astype(BF16)
                spick = jnp.where(scol == lanes, 1.0, 0.0).astype(BF16)
                from_recv = dot(rpick, cat[trecv_ref[tile]])
                from_send = dot(spick, slat_ref[tsend_ref[tile]])
                recv_rows.append(from_recv[:, 0:width].astype(BF16))
                send_rows.append(from_send.astype(BF16))
                flat = grad_ref[t].astype(F32)
                least = jnp.where(tile < count, 0, block)
                weighted.append(jnp.where(rcol >= least, flat + from_recv[:, width:], 0.0))
                flats.append(flat)
                picks.append(jnp.concatenate([rpick, spick], axis=1))
            edges = edge_ref[pair * PAIR:(pair + 1) * PAIR].reshape(PAIR * slots, width)
            inputs = jnp.concatenate(
                [edges, jnp.concatenate(recv_rows, axis=0), jnp.concatenate(send_rows, axis=0)],
                axis=1)
            pre = dot(inputs, first)
            hidden = jnp.maximum(pre, 0.0).astype(BF16)
            raw = dot(hidden, second_ref[...])
            grad_raw, gain_term = norm_back(raw, jnp.concatenate(weighted, axis=0), gain)
            acc_gain[...] += jnp.sum(gain_term.reshape(-1, 8, width), axis=0)
            grad_hidden = dot(grad_raw, second_t[...])
            grad_pre = jnp.where(pre > 0.0, grad_hidden, 0.0).astype(BF16)
            acc_second[...] += dot(hidden.T, grad_raw)
            grad_in = dot(grad_pre, first_t[...])
            grad_pre_t = grad_pre.T
            acc_first[:, 0:width] += dot(grad_pre_t, edges)
            for i in range(PAIR):
                t = pair * PAIR + i
                tile = step * GROUP + t
                out_ref[t] = (flats[i] + grad_in[i * slots:(i + 1) * slots]).astype(BF16)
                both = dot(grad_pre_t[:, i * slots:(i + 1) * slots], picks[i])
                acc_r[trecv_ref[tile]] += both[:, 0:block]
                acc_s[tsend_ref[tile]] += both[:, block:]

    @pl.when(step == pl.num_programs(0) - 1)
    def _():
        half = block // 2
        recv_w = first_ref[width:2 * width, :]
        send_w = first_ref[2 * width:3 * width, :]
        first_r = acc_first[:, width:2 * width]
        for b in range(nr):
            summed = acc_r[b].astype(BF16)
            total = dot(recv_w, summed).T.astype(BF16)
            first_r += dot(summed, rlat_ref[b])
            for h in range(2):
                pack_ref[h, b * half:(b + 1) * half, :] = total[h * half:(h + 1) * half]
        first_s = acc_first[:, 2 * width:3 * width]
        for b in range(nc):
            summed = acc_s[b].astype(BF16)
            total = dot(send_w, summed).T.astype(BF16)
            first_s += dot(summed, slat_ref[b])
            for h in range(2):
                pack_ref[h, (nr + b) * half:(nr + b + 1) * half, :] = total[h * half:(h + 1) * half]
        w0 = (nr + nc) * half
        hid = second_ref.shape[0]
        pack_ref[0, w0:w0 + width, :] = acc_first[:, 0:width].T.astype(BF16)
        pack_ref[0, w0 + width:w0 + 2 * width, :] = first_r.T.astype(BF16)
        pack_ref[0, w0 + 2 * width:w0 + 3 * width, :] = first_s.T.astype(BF16)
        pack_ref[0, w0 + 3 * width:w0 + 3 * width + hid, :] = acc_second[...].astype(BF16)
        used = 3 * width + hid
        if half_rows > used:
            pack_ref[0, w0 + used:w0 + half_rows, :] = jnp.zeros((half_rows - used, width), BF16)
        nw = wn_ref.shape[0]
        pack_ref[1, w0:w0 + nw, :] = wn_ref[...]
        pack_ref[1, w0 + nw:w0 + nw + 16, :] = jnp.broadcast_to(
            jnp.sum(acc_gain[...], axis=0, keepdims=True), (16, width)).astype(BF16)
        pack_ref[1, w0 + nw + 16:w0 + half_rows, :] = jnp.zeros(
            (half_rows - nw - 16, width), BF16)


def sum_kernel(
    nr, nc, chunk, pack_ref, base_ref,
    glat_ref, wfin,
    buf, part, rbuf, sbuf, wbuf,
    p_send, p_recv, w_send, w_recv, r_send, r_recv, s_send, s_recv,
    a_send, a_recv, f_send, f_recv,
):
    row, col, rep = lax.axis_index("row"), lax.axis_index("col"), lax.axis_index("rep")
    chips = nr * nc
    here = row * nc + col
    other_rep = 1 - rep
    rows = base_ref.shape[0]
    w0 = (nr + nc) * rows
    half_rows = chunk * chips
    twin = {"rep": other_rep}

    def chip(k):
        other = lax.rem(here + k, chips)
        return other, {"row": lax.div(other, nc), "col": lax.rem(other, nc)}

    barrier = pltpu.get_barrier_semaphore()
    pl.semaphore_signal(barrier, inc=1, device_id=twin, device_id_type=MESH)
    for k in range(1, chips):
        pl.semaphore_signal(barrier, inc=1, device_id=chip(k)[1], device_id_type=MESH)
    pl.semaphore_wait(barrier, chips)

    def send(src, dst, send_sem, recv_sem, device):
        copy = pltpu.make_async_remote_copy(
            src_ref=src, dst_ref=dst, send_sem=send_sem, recv_sem=recv_sem,
            device_id=device, device_id_type=MESH)
        copy.start()
        return copy

    w_part, n_part = pl.ds(w0, half_rows), pl.ds(0, w0)
    p_w = send(pack_ref.at[other_rep, w_part], buf.at[w_part], p_send.at[0], p_recv.at[0], twin)
    p_n = send(pack_ref.at[other_rep, n_part], buf.at[n_part], p_send.at[1], p_recv.at[1], twin)

    def at_chunk(index):
        return pl.ds(pl.multiple_of(index * chunk, 16), chunk)

    def at_part(offset, index, size):
        return pl.ds(pl.multiple_of(offset + index * size, 16), size)

    p_w.wait_recv()
    part[w_part, :] = (pack_ref[rep, w_part, :].astype(F32) + buf[w_part, :].astype(F32)).astype(BF16)
    w_copies = []
    for k in range(1, chips):
        other, device = chip(k)
        w_copies.append(send(part.at[at_part(w0, other, chunk)], wbuf.at[k],
                             w_send.at[k], w_recv.at[k], device))
    p_n.wait_recv()
    part[n_part, :] = (pack_ref[rep, n_part, :].astype(F32) + buf[n_part, :].astype(F32)).astype(BF16)
    r_copies, s_copies = [], []
    for k in range(1, nr):
        other = lax.rem(row + k, nr)
        r_copies.append(send(part.at[at_part(0, other, rows)], rbuf.at[k],
                             r_send.at[k], r_recv.at[k], {"row": other}))
    for k in range(1, nc):
        other = lax.rem(col + k, nc)
        s_copies.append(send(part.at[at_part(nr * rows, other, rows)], sbuf.at[k],
                             s_send.at[k], s_recv.at[k], {"col": other}))

    total = part[at_part(w0, here, chunk), :].astype(F32)
    for k in range(1, chips):
        w_copies[k - 1].wait_recv()
        total += wbuf[k].astype(F32)
    wfin[rep, at_chunk(here), :] = total.astype(BF16)
    mine = wfin.at[rep, at_chunk(here)]
    a_copies = [send(mine, mine, a_send.at[k], a_recv.at[k], chip(k)[1]) for k in range(1, chips)]
    f_copies = [send(mine, mine, f_send.at[0], f_recv.at[0], twin)]

    grads = base_ref[...] + part[at_part(0, row, rows), :].astype(F32)
    grads += part[at_part(nr * rows, col, rows), :].astype(F32)
    for k in range(1, nr):
        r_copies[k - 1].wait_recv()
        grads += rbuf[k].astype(F32)
    for k in range(1, nc):
        s_copies[k - 1].wait_recv()
        grads += sbuf[k].astype(F32)
    glat_ref[...] = grads.astype(BF16)

    for k in range(1, chips):
        a_copies[k - 1].wait_recv()
        source = lax.rem(here + chips - k, chips)
        passed = wfin.at[rep, at_chunk(source)]
        f_copies.append(send(passed, passed, f_send.at[k], f_recv.at[k], twin))
    for copy in f_copies:
        copy.wait_recv()
    for copy in [p_w, p_n] + w_copies + r_copies + s_copies + a_copies + f_copies:
        copy.wait_send()


def write_kernel(
    glat_ref, wfin, glat_out, ef_out, es_out, eg_out, nf_out, ns_out, ng_out,
    ef_ref, es_ref, eg_ref, nf_ref, ns_ref, ng_ref, sems,
):
    def store(i, src, dst):
        copy = pltpu.make_async_copy(src, dst, sems.at[i])
        copy.start()
        return copy

    copies = [store(0, glat_ref, glat_out)]
    nef, nes = ef_ref.shape[0], es_ref.shape[0]
    ef_ref[...] = wfin[0, 0:nef, :].astype(F32)
    copies.append(store(1, ef_ref, ef_out))
    es_ref[...] = wfin[0, nef:nef + nes, :].astype(F32)
    copies.append(store(2, es_ref, es_out))
    nnf, nns = nf_ref.shape[0], ns_ref.shape[0]
    nf_ref[...] = wfin[1, 0:nnf, :].astype(F32)
    copies.append(store(3, nf_ref, nf_out))
    ns_ref[...] = wfin[1, nnf:nnf + nns, :].astype(F32)
    copies.append(store(4, ns_ref, ns_out))
    gains = wfin[1, nnf + nns:nnf + nns + 32, :].astype(F32)
    ng_ref[...] = gains[0:1]
    eg_ref[...] = gains[16:17]
    copies.append(store(5, ng_ref, ng_out))
    copies.append(store(6, eg_ref, eg_out))
    for copy in copies:
        copy.wait()


def per_device(
    latents, saved_sum, grad_latents_out, edge_latents, grad_edges_out, recv_slot, send_slot,
    tile_recv, tile_send, tile_count, edge_first, edge_second, edge_gain,
    node_first, node_second, node_gain,
):
    nr, nc = lax.axis_size("row"), lax.axis_size("col")
    rows, width = latents.shape
    tiles, slots, _ = edge_latents.shape
    block = rows * 2
    chips = nr * nc
    vmem = pl.BlockSpec(memory_space=pltpu.VMEM)
    hbm = pl.BlockSpec(memory_space=pl.ANY)
    dma = pltpu.SemaphoreType.DMA
    weight_rows = edge_first.shape[0] + edge_second.shape[0]
    node_rows = node_first.shape[0] + node_second.shape[0]
    chunk = -(-max(weight_rows, node_rows + 32) // (16 * chips)) * 16
    half_rows = chunk * chips
    shape = jax.ShapeDtypeStruct

    rlat, rgrad, slat, base, wn = pl.pallas_call(
        functools.partial(node_kernel, nr, nc),
        out_shape=(
            shape((nr * block, width), BF16), shape((nr * block, width), BF16),
            shape((nc * block, width), BF16), shape((rows, width), F32),
            shape((node_rows + 16, width), BF16),
        ),
        in_specs=[hbm] * 6,
        out_specs=(vmem,) * 5,
        scratch_shapes=[
            pltpu.VMEM((rows, width), BF16), pltpu.VMEM((rows, width), BF16),
            pltpu.VMEM((rows, width), BF16), pltpu.VMEM(node_first.shape, BF16),
            pltpu.VMEM(node_second.shape, BF16), pltpu.VMEM((1, width), F32),
            pltpu.VMEM((rows, width), BF16), dma((6,)),
        ] + [dma((nr,))] * 8 + [dma((nc,))] * 4,
        compiler_params=pltpu.CompilerParams(
            collective_id=0, has_side_effects=True, vmem_limit_bytes=LIMIT),
    )(latents, saved_sum, grad_latents_out, node_first, node_second, node_gain.reshape(1, -1))

    def whole(*dims):
        return pl.BlockSpec(dims, lambda i, *_: (0,) * len(dims))

    tiled = pl.BlockSpec((GROUP, slots, width), lambda i, *_: (i, 0, 0))
    slotted = pl.BlockSpec((GROUP, slots), lambda i, *_: (i, 0))
    pack_rows = (nr + nc) * rows + half_rows
    grads_out, pack = pl.pallas_call(
        functools.partial(edge_kernel, nr, nc, half_rows),
        out_shape=(shape(edge_latents.shape, BF16), shape((2, pack_rows, width), BF16)),
        grid_spec=pltpu.PrefetchScalarGridSpec(
            num_scalar_prefetch=3,
            grid=(tiles // GROUP,),
            in_specs=[
                tiled, tiled, slotted, slotted,
                whole(nr, block, width), whole(nr, block, width), whole(nc, block, width),
                whole(*edge_first.shape), whole(*edge_second.shape), whole(1, width),
                whole(node_rows + 16, width),
            ],
            out_specs=(tiled, whole(2, pack_rows, width)),
            scratch_shapes=[
                pltpu.VMEM((nr, block, 2 * width), BF16),
                pltpu.VMEM((edge_first.shape[1], width), BF16),
                pltpu.VMEM((width, edge_second.shape[0]), BF16),
                pltpu.VMEM((nr, edge_first.shape[1], block), F32),
                pltpu.VMEM((nc, edge_first.shape[1], block), F32),
                pltpu.VMEM((edge_first.shape[1], edge_first.shape[0]), F32),
                pltpu.VMEM(edge_second.shape, F32),
                pltpu.VMEM((8, width), F32),
            ],
        ),
        compiler_params=pltpu.CompilerParams(
            dimension_semantics=("arbitrary",), vmem_limit_bytes=LIMIT),
    )(
        tile_recv, tile_send, tile_count, edge_latents, grad_edges_out, recv_slot, send_slot,
        rlat.reshape(nr, block, width), rgrad.reshape(nr, block, width),
        slat.reshape(nc, block, width), edge_first, edge_second, edge_gain.reshape(1, -1), wn,
    )

    glat, totals = pl.pallas_call(
        functools.partial(sum_kernel, nr, nc, chunk),
        out_shape=(shape((rows, width), BF16), shape((2, half_rows, width), BF16)),
        in_specs=[vmem] * 2,
        out_specs=(vmem,) * 2,
        scratch_shapes=[
            pltpu.VMEM((pack_rows, width), BF16), pltpu.VMEM((pack_rows, width), BF16),
            pltpu.VMEM((nr, rows, width), BF16), pltpu.VMEM((nc, rows, width), BF16),
            pltpu.VMEM((chips, chunk, width), BF16),
            dma((2,)), dma((2,)), dma((chips,)), dma((chips,)), dma((nr,)), dma((nr,)),
            dma((nc,)), dma((nc,)), dma((chips,)), dma((chips,)), dma((chips,)), dma((chips,)),
        ],
        compiler_params=pltpu.CompilerParams(
            collective_id=1, has_side_effects=True, vmem_limit_bytes=24 << 20),
    )(pack, base)
    finals = (
        shape(edge_first.shape, F32), shape(edge_second.shape, F32), shape((1, width), F32),
        shape(node_first.shape, F32), shape(node_second.shape, F32), shape((1, width), F32),
    )
    outs = pl.pallas_call(
        write_kernel,
        out_shape=(shape((rows, width), BF16),) + finals,
        in_specs=[vmem] * 2,
        out_specs=(hbm,) * 7,
        scratch_shapes=[pltpu.VMEM(item.shape, F32) for item in finals] + [dma((7,))],
        compiler_params=pltpu.CompilerParams(vmem_limit_bytes=24 << 20),
    )(glat, totals)
    grad_latents, ef, es, eg, nf, ns, ng = outs
    return (grad_latents, grads_out, ef, es, eg.reshape(-1), nf, ns, ng.reshape(-1))


def solution(mesh):
    spread = ("groups", "row", "col", "rep")
    two, three, one = P(spread, None), P(spread, None, None), P(spread)
    in_specs = (two, two, two, three, three, two, two, one, one, one) + (P(),) * 6
    out_specs = (
        two, three, P("groups", None), P("groups", None), P("groups"),
        P("groups", None), P("groups", None), P("groups"),
    )
    return jax.shard_map(
        per_device, mesh=mesh, in_specs=in_specs, out_specs=out_specs, check_vma=False
    )
```
